256 devices in a mesh: user: 32 (over z, x), tp: 8 (over y, core).
Axes of the slice: x: 4, y: 4, z: 8, core: 2. Of those that a mesh axis runs over, the one named last changes fastest.
Arguments:
- cand_feats: bfloat16 [32768, 1024], P('user', 'tp'), may hold values from -6 to 6
- w_in: bfloat16 [1024, 2048], P(None, 'tp'), may hold values from -0.1875 to 0.1875
- w_out: bfloat16 [1024, 1024], P('tp'), may hold values from -0.1875 to 0.1875
- kv_cache: bfloat16 [2048, 128, 2048], P('user', None, 'tp'), may hold values from -6 to 6
- event_mask: int32 [2048, 128], P('user'), may hold values from 0 to 1, as said below
- block_counts: int32 [256], P('user'), may hold values from 1 to 8, as said below
- user_blocks: int32 [256, 8], P('user'), may hold values from 0 to 63, as said below
- send_slots: int32 [1024, 2], P('user'), may hold values from 0 to 63, as said below
- cand_user: int32 [32768], P('user'), may hold values from 0 to 7
Outputs:
- scored: bfloat16 [32768, 1024], P('user', 'tp')
The draws below stay inside these ranges and needn't reach their ends.
Inputs may be any that keep to these rules, and one draw needn't show every extreme that they name: `block_counts`: on every index of the user axis some user has 8 blocks, and on one index every user has. For user u of the index r of the user axis and j < block_counts[r * 8 + u], user_blocks[r * 8 + u, j] = o * 2 + c says that block j of u's history is cached on index o, in its local row send_slots[o * 32 + r, c] of kv_cache and event_mask. These valid entries of one index's users are all different, and on one index they take all 64 values. Entries with j >= block_counts[u] are arbitrary. `send_slots`: the 32 rows of one holder o (rows o * 32 to o * 32 + 31) name each of its local rows 0 to 63 exactly once. `event_mask`: in every block of a user's history the first event is real.
All inputs are finite; a program needn't handle non-finite values.
Results may differ from the reference program's by a relative error of at most 0.013.
Values may be sent and summed in bfloat16 or wider, within the bound.
A program may use at most 128 MiB of HBM per device.

```python
import jax
import jax.numpy as jnp
from jax import lax

D = 1024
H = 8
DH = 128
EVENTS = 128
MAXB = 8
USERS_DEV = 8
CAND_DEV = 1024
CAP = 2
SLOTS = 64
BLOCKS = 2048
CANDS = 32768
N_USER = 32


def shuffle_peers(subkey):
    return jax.random.permutation(subkey, N_USER)


def shuffle_slots(subkey):
    return jax.random.permutation(subkey, SLOTS)


def make_tables(key):
    base_key = jax.random.fold_in(key, 4243)
    keyset = jax.random.split(base_key, 10)
    peer_count = N_USER
    most_blocks = MAXB
    draw_first = jax.random.randint(keyset[0], (peer_count, USERS_DEV), 1, most_blocks + 1)
    draw_second = jax.random.randint(keyset[1], (peer_count, USERS_DEV), 1, most_blocks + 1)
    counts = (draw_first * draw_second + most_blocks - 1) // most_blocks
    full_user = jax.random.randint(keyset[2], (peer_count,), 0, USERS_DEV)
    user_ids = jnp.arange(USERS_DEV)
    counts = jnp.where(user_ids[None, :] == full_user[:, None], most_blocks, counts)
    full_rank = jax.random.randint(keyset[3], (), 0, peer_count)
    counts = jnp.where(jnp.arange(peer_count)[:, None] == full_rank, most_blocks, counts)
    offsets = jnp.cumsum(counts, axis=1) - counts
    block_pos = jnp.arange(most_blocks)
    sequence_no = offsets[:, :, None] + block_pos[None, None, :]
    in_use = block_pos[None, None, :] < counts[:, :, None]
    spreads = jax.vmap(shuffle_peers)(jax.random.split(keyset[4], peer_count))
    owners = jnp.take_along_axis(spreads, (sequence_no % peer_count).reshape(peer_count, -1), axis=1).reshape(sequence_no.shape)
    places = sequence_no // peer_count
    garbage = jax.random.randint(keyset[5], sequence_no.shape, 0, peer_count * CAP)
    blocks_table = jnp.where(in_use, owners * CAP + places, garbage)
    slot_perm = jax.vmap(shuffle_slots)(jax.random.split(keyset[6], peer_count))
    last_len = jax.random.randint(keyset[7], (peer_count, USERS_DEV), 1, EVENTS + 1)
    lengths = jnp.where(block_pos[None, None, :] == counts[:, :, None] - 1, last_len[:, :, None], EVENTS)
    events = jnp.arange(EVENTS)
    hole_draw = jax.random.randint(keyset[8], sequence_no.shape + (EVENTS,), 0, 4)
    kept_mask = ((events < lengths[..., None]) & ((hole_draw > 0) | (events == 0))).astype(jnp.int32)
    filler = jax.random.randint(keyset[9], (peer_count, peer_count, CAP, EVENTS), 0, 2)
    rank_ids = jnp.broadcast_to(jnp.arange(peer_count)[:, None, None], sequence_no.shape)
    target = jnp.where(in_use, places, CAP)
    mask_grid = filler.at[rank_ids, owners, target].set(kept_mask, mode='drop')
    by_owner = jnp.transpose(mask_grid, (1, 0, 2, 3)).reshape(peer_count, SLOTS, EVENTS)
    mask_rows = jnp.zeros((peer_count, SLOTS, EVENTS), jnp.int32).at[jnp.arange(peer_count)[:, None], slot_perm].set(by_owner)
    return (counts.reshape(-1).astype(jnp.int32), blocks_table.reshape(peer_count * USERS_DEV, most_blocks).astype(jnp.int32), slot_perm.reshape(peer_count * peer_count, CAP).astype(jnp.int32), mask_rows.reshape(peer_count * SLOTS, EVENTS).astype(jnp.int32))


def draw_block_counts(key, part):
    return make_tables(key)[0]


def draw_user_blocks(key, part):
    return make_tables(key)[1]


def draw_send_slots(key, part):
    return make_tables(key)[2]


def draw_event_mask(key, part):
    return make_tables(key)[3]


def set_ends(array, rng, low, largest):
    longest = array.shape.index(max(array.shape))
    spots = []
    for shift in (0, 1):
        where = [jax.random.randint(jax.random.fold_in(rng, axis), (), 0, length) for axis, length in enumerate(array.shape)]
        where[longest] = (where[longest] + shift) % array.shape[longest]
        spots.append(tuple(where))
    return array.at[spots[0]].set(low).at[spots[1]].set(largest)


def steps_of(own_key, dims, pieces, smallest, high):
    loudness, own = 1.0, jax.random.fold_in(own_key, 6)
    for position, blocks in pieces:
        draws = jnp.exp(jax.random.uniform(jax.random.fold_in(own, position), (blocks,), jnp.float32, smallest / len(pieces), high / len(pieces)))
        loudness = loudness * jnp.repeat(draws, dims[position] // blocks).reshape([-1 if axis == position else 1 for axis in range(len(dims))])
    return loudness


def noise(rng, shape, width, reach, pieces=(), held_as=jnp.bfloat16):
    loudness = steps_of(rng, shape, pieces, -0.22, 0.18) if pieces else 1.0
    values = jax.random.normal(rng, shape, jnp.float32) * width * loudness
    return jnp.minimum(jnp.maximum(values, -reach), reach).astype(held_as)


def setup_inputs(seed: int = 0) -> dict:
    key_list = jax.random.split(jax.random.key(seed), 10)
    cand_feats = noise(key_list[0], (CANDS, D), 1.0, 6.0, ((0, 32), (1, 8)))
    w_in = noise(key_list[1], (D, 2 * D), D ** -0.5, 0.1875, ((1, 8),))
    w_out = noise(key_list[2], (D, D), D ** -0.5, 0.1875, ((0, 8),))
    kv_cache = noise(key_list[3], (BLOCKS, EVENTS, 2 * D), 1.0, 6.0, ((0, 32), (2, 8)))
    event_mask = draw_event_mask(jax.random.fold_in(key_list[9], 71), 0)
    block_counts = draw_block_counts(jax.random.fold_in(key_list[9], 71), 0)
    user_blocks = draw_user_blocks(jax.random.fold_in(key_list[9], 71), 0)
    send_slots = draw_send_slots(jax.random.fold_in(key_list[9], 71), 0)
    cand_user = set_ends(jax.random.randint(key_list[8], (CANDS,), 0, USERS_DEV), jax.random.fold_in(key_list[8], 1), 0, USERS_DEV - 1).astype(jnp.int32)
    return {"cand_feats": cand_feats, "w_in": w_in, "w_out": w_out, "kv_cache": kv_cache, "event_mask": event_mask, "block_counts": block_counts, "user_blocks": user_blocks, "send_slots": send_slots, "cand_user": cand_user}


norm_eps = 1e-06

def owner_users(block_count, block_table, slot_count):
    user_count, most_blocks = block_table.shape
    live_mask = jnp.arange(most_blocks, dtype=jnp.int32)[None, :] < block_count[:, None]
    slot_hit = (block_table[:, :, None] == jnp.arange(slot_count, dtype=jnp.int32)[None, None, :]) & live_mask[:, :, None]
    user_label = jnp.arange(user_count, dtype=jnp.int32)[:, None, None] + 1
    return (lax.optimization_barrier(jnp.sum(jnp.where(slot_hit, user_label, 0), axis=(0, 1))) - 1).astype(jnp.int32)

def attend_ref(queries, cand_users, key_rows, value_rows, live_mask, slot_users):
    block_rows = min(512, CAND_DEV)
    key_float = key_rows.astype(jnp.float32)
    value_float = value_rows.astype(jnp.float32)

    def one_block(packed):
        query_block, user_block = packed
        same_user = (user_block[:, None] == slot_users[None, :]).astype(jnp.float32)
        weights = (same_user[:, :, None] * live_mask[None]).reshape(query_block.shape[0], -1)
        scores = jnp.einsum('rhd,ehd->hre', query_block.astype(jnp.float32), key_float) * DH ** (-0.5)
        attn_weights = (jax.nn.silu(scores) * weights[None]).astype(jnp.bfloat16)
        return jnp.einsum('hre,ehd->rhd', attn_weights.astype(jnp.float32), value_float)
    result = lax.map(one_block, (queries.reshape(-1, block_rows, H, DH), cand_users.reshape(-1, block_rows)))
    return result.reshape(-1, H, DH)

def reference(cand_feats, w_in, w_out, kv_cache, event_mask, block_counts, user_blocks, send_slots, cand_user):
    slot_total = N_USER * CAP
    slot_table = send_slots.reshape(N_USER, N_USER, CAP)

    def ranker(ranker_index):
        features = lax.dynamic_slice_in_dim(cand_feats, ranker_index * CAND_DEV, CAND_DEV, 0)
        users_here = lax.dynamic_slice_in_dim(cand_user, ranker_index * CAND_DEV, CAND_DEV, 0)
        counts_here = lax.dynamic_slice_in_dim(block_counts, ranker_index * USERS_DEV, USERS_DEV, 0)
        table_here = lax.dynamic_slice_in_dim(user_blocks, ranker_index * USERS_DEV, USERS_DEV, 0)
        projected = jnp.dot(features, w_in, preferred_element_type=jnp.float32)
        activated = jax.nn.silu(projected).reshape(CAND_DEV, H, 2, DH)
        queries = activated[:, :, 0, :].astype(jnp.bfloat16)
        gates = activated[:, :, 1, :].astype(jnp.bfloat16)
        picked = jnp.take(slot_table, ranker_index, axis=1).astype(jnp.int32)
        global_rows = (jnp.arange(N_USER, dtype=jnp.int32)[:, None] * SLOTS + picked).reshape(-1).astype(jnp.int32)
        blocks_here = kv_cache[global_rows].reshape(slot_total * EVENTS, H, 2, DH)
        live_mask = event_mask[global_rows].astype(jnp.float32)
        slot_users = owner_users(counts_here, table_here, slot_total)
        attended = attend_ref(queries, users_here, blocks_here[:, :, 0, :], blocks_here[:, :, 1, :], live_mask, slot_users)
        normed = attended * lax.rsqrt(lax.optimization_barrier(jnp.mean(attended * attended, axis=-1, keepdims=True)) + norm_eps) * gates.astype(jnp.float32)
        hidden = normed.astype(jnp.bfloat16).reshape(CAND_DEV, H * DH)
        mixed = jnp.dot(hidden, w_out, preferred_element_type=jnp.float32)
        return (features.astype(jnp.float32) + mixed).astype(jnp.bfloat16)
    scored = lax.map(ranker, jnp.arange(N_USER, dtype=jnp.int32))
    return scored.reshape(CANDS, D)
```

```python
import functools

import jax
import jax.numpy as jnp
from jax import lax
from jax.experimental import pallas as pl
from jax.experimental.pallas import tpu as pltpu
from jax.sharding import PartitionSpec as P

DH = 128
EVENTS = 128
CAP = 2
CORES = 2
Z_SIZE = 8
norm_eps = 1e-06
FAR = -float(2**30)
HALF_SCALE = 0.5 * DH**-0.5
MESH = pl.DeviceIdType.MESH


def silu(v):
    x = 0.5 * v
    return x + x * jnp.tanh(x)


def kernel(
    dims,
    slots_ref,
    info_ref,
    mask_ref,
    kv_hbm,
    feats_hbm,
    w_in_hbm,
    w_out_hbm,
    out_ref,
    kv_v,
    snd,
    kvr,
    feats,
    w_in_v,
    w_out_v,
    w_out_all,
    info_all,
    qs,
    gates,
    onehot,
    parts,
    incoming,
    att,
    hid,
    loc_sem,
    x_ss,
    x_rs,
    info_ss,
    info_rs,
    f_ss,
    f_rs,
    h_ss,
    h_rs,
    w_ss,
    w_rs,
    q_ss,
    q_rs,
    p_ss,
    p_rs,
):
    nz, nx, ny = dims
    far = nz // 2
    half = feats.shape[2]
    n_tp = ny * CORES
    n_blk = nx * CAP
    me_u = lax.axis_index("user")
    me_t = lax.axis_index("tp")
    z, x = me_u // nx, me_u % nx
    y, core = me_t // CORES, me_t % CORES

    def at_z(d):
        return ((z + d + nz) % nz * nx + x, me_t)

    def at_x(j):
        return (z * nx + (x + j) % nx, me_t)

    def at_t(t):
        return (me_u, t)

    def rc(src, dst, ss, rs, dev):
        return pltpu.make_async_remote_copy(
            src_ref=src, dst_ref=dst, send_sem=ss, recv_sem=rs,
            device_id=dev, device_id_type=MESH,
        )

    kv_load = pltpu.make_async_copy(kv_hbm, kv_v, loc_sem.at[0])
    wi_load = pltpu.make_async_copy(w_in_hbm, w_in_v, loc_sem.at[1])
    wo_load = pltpu.make_async_copy(w_out_hbm, w_out_v, loc_sem.at[2])
    f_loads = [
        pltpu.make_async_copy(feats_hbm.at[h], feats.at[me_t, h], loc_sem.at[3 + h])
        for h in range(2)
    ]
    for load in f_loads:
        load.start()
    kv_load.start()
    wi_load.start()
    wo_load.start()

    barrier = pltpu.get_barrier_semaphore()
    peers = [at_z(d) for d in range(1, nz)]
    peers += [at_x(j) for j in range(1, nx)]
    peers += [at_t((me_t + j) % n_tp) for j in range(1, n_tp)]
    for dev in peers:
        pl.semaphore_signal(barrier, inc=1, device_id=dev, device_id_type=MESH)
    onehot[...] = jnp.zeros_like(onehot)
    info_all[0] = info_ref[z]
    pl.semaphore_wait(barrier, len(peers))

    sends = []

    def go(copy):
        copy.start()
        sends.append(copy)

    partner = y * CORES + 1 - core

    def y_src(j, c):
        return (y - j + ny) % ny * CORES + c

    def y_send(buf, h, ss, rs):
        own = buf.at[me_t, h]
        for j in range(1, ny):
            go(rc(own, own, ss.at[h, j], rs.at[h, j], at_t((y + j) % ny * CORES + core)))
        go(rc(own, own, ss.at[h, 0], rs.at[h, 0], at_t(partner)))

    def y_forward(buf, h, ss, rs):
        for j in range(1, ny):
            got = buf.at[y_src(j, core), h]
            rc(got, got, ss.at[h, j], rs.at[h, j], at_t(partner)).wait_recv()
            k = ny - 1 + j
            go(rc(got, got, ss.at[h, k], rs.at[h, k], at_t(partner)))

    def y_wait(buf, h, ss, rs):
        for j in range(ny):
            k = 0 if j == 0 else ny - 1 + j
            got = buf.at[y_src(j, 1 - core), h]
            rc(got, got, ss.at[h, k], rs.at[h, k], at_t(partner)).wait_recv()

    for h in range(2):
        f_loads[h].wait()
        y_send(feats, h, f_ss, f_rs)
    for d in range(1, nz):
        go(rc(info_ref.at[(z + d) % nz], info_all.at[d], info_ss.at[d], info_rs.at[d], at_z(d)))

    def prepare(k):
        ranker = (z - k + nz) % nz * nx

        def one(i, carry):
            j, c = i // CAP, i % CAP
            slot = slots_ref[ranker + (x + j) % nx, c]
            block = kv_v[slot]
            live = mask_ref[slot].astype(jnp.float32).astype(jnp.bfloat16)
            snd[k, j, c, :, 0:DH] = block[:, 0:DH]
            snd[k, j, c, :, DH:] = block[:, DH:].T * live
            return carry

        lax.fori_loop(0, n_blk, one, 0)
        for j in range(1, nx):
            go(rc(snd.at[k, j], kvr.at[k, j], x_ss.at[k, j], x_rs.at[k, j], at_x(j)))

    def q_slot(way, d):
        return way * far + d if d else 0

    def project(h):
        rows = jnp.concatenate([feats[t, h] for t in range(n_tp)], axis=1)
        act = silu(jnp.dot(rows, w_in_v[...], preferred_element_type=jnp.float32))
        qs[0, h] = act[:, 0:DH].T.astype(jnp.bfloat16)
        gates[h] = act[:, DH:].astype(jnp.bfloat16)

    def q_copy(way, d, h):
        return rc(
            qs.at[q_slot(way, d - 1), h], qs.at[q_slot(way, d), h],
            q_ss.at[way, d, h], q_rs.at[way, d, h], at_z(1 if way == 0 else -1),
        )

    def q_ways(d, h):
        return [w for w in range(2) if d < far or w == h] if d <= far else []

    order = [far]
    for d in range(far - 1, 0, -1):
        order += [d, nz - d]
    order += [0]

    kv_load.wait()
    todo = list(order)
    prepare(todo.pop(0))
    y_forward(feats, 0, f_ss, f_rs)
    if todo:
        prepare(todo.pop(0))
    y_forward(feats, 1, f_ss, f_rs)
    wi_load.wait()
    y_wait(feats, 0, f_ss, f_rs)
    project(0)
    for way in q_ways(1, 0):
        go(q_copy(way, 1, 0))
    y_wait(feats, 1, f_ss, f_rs)
    project(1)
    for way in q_ways(1, 1):
        go(q_copy(way, 1, 1))
    wo_load.wait()
    w_out_all[me_t] = w_out_v[:, pl.ds(pl.multiple_of(me_t * DH, DH), DH)]
    for j in range(1, n_tp):
        t = (me_t + j) % n_tp
        cols = pl.ds(pl.multiple_of(t * DH, DH), DH)
        go(rc(w_out_v.at[:, cols], w_out_all.at[me_t], w_ss.at[j], w_rs.at[j], at_t(t)))
    for d in range(1, far):
        for h in range(2):
            if todo:
                prepare(todo.pop(0))
            for way in q_ways(d, h):
                q_copy(way, d, h).wait_recv()
                if way in q_ways(d + 1, h):
                    go(q_copy(way, d + 1, h))
    while todo:
        prepare(todo.pop(0))

    def p_copy(way, d, h):
        to = (z + 2 * way - 1 + nz) % nz * nx + x
        return rc(
            parts.at[way, d - 1, h], incoming.at[way, d - 1, h],
            p_ss.at[way, d - 1, h], p_rs.at[way, d - 1, h], (to, me_t),
        )

    def attend(k, q, h):
        user = lax.broadcasted_iota(jnp.int32, (16, DH), 0).astype(jnp.float32)
        for i in range(half // DH):
            row = info_all[k, pl.ds(h * (half // DH) + i, 1), :]
            onehot[0:16, i * DH : (i + 1) * DH] = jnp.where(row == user, 1.0, 0.0).astype(jnp.bfloat16)
        keys, values = [], []
        for j in range(nx):
            for c in range(CAP):
                block = snd[k, 0, c] if j == 0 else kvr[k, j, c]
                b = (x - j + nx) % nx * CAP + c
                ext = info_all[k, pl.ds(8 + b, 1), :].astype(jnp.bfloat16)
                ext = jnp.broadcast_to(ext, (EVENTS, DH))
                keys.append(jnp.concatenate([block[:, 0:DH], ext], axis=1))
                values.append(block[:, DH:])
        rhs = jnp.concatenate([qs[q, h], onehot[...]], axis=0)
        v = HALF_SCALE * jnp.dot(
            jnp.concatenate(keys, axis=0), rhs, preferred_element_type=jnp.float32
        )
        w = (v + v * jnp.tanh(v)).astype(jnp.bfloat16)
        return jnp.dot(jnp.concatenate(values, axis=1), w, preferred_element_type=jnp.float32)

    def wait_blocks(k):
        for j in range(1, nx):
            rc(snd.at[k, j], kvr.at[k, j], x_ss.at[k, j], x_rs.at[k, j], at_x(j)).wait_recv()

    def wait_info(k):
        rc(info_ref.at[0], info_all.at[k], info_ss.at[k], info_rs.at[k], at_z(1)).wait_recv()

    def one_task(i, carry):
        d = far - (i + 2) // 4
        r = (i + 2) % 4
        at_far = d // far
        way = r % 2
        h = (1 - at_far) * (r // 2) + at_far * (r % 2)
        k = (d + way * (nz - 2 * d)) % nz
        first = (1 - at_far) * (r // 2) + at_far * way

        @pl.when(jnp.logical_and(first == 0, d > 0))
        def _():
            wait_blocks(k)
            wait_info(k)

        @pl.when(jnp.logical_and(r == 0, d == 0))
        def _():
            wait_blocks(k)

        @pl.when(d == far)
        def _():
            rc(
                qs.at[0, h], qs.at[way * far + d, h], q_ss.at[way, d, h], q_rs.at[way, d, h], at_z(1)
            ).wait_recv()

        own = (d + far - 1) // far
        hh = own * h + (1 - own) * way
        total = attend(k, own * (way * far + d), hh)

        @pl.when(d == 0)
        def _():
            att[hh] = total

        @pl.when(jnp.logical_and(d > 0, jnp.logical_or(d == far, jnp.logical_and(d == far - 1, h != way))))
        def _():
            parts[way, d - 1, h] = total.astype(jnp.bfloat16)

        @pl.when(jnp.logical_and(d > 0, jnp.logical_or(d < far - 1, jnp.logical_and(d == far - 1, h == way))))
        def _():
            p_copy(way, d + 1, h).wait_recv()
            parts[way, d - 1, h] = (total + incoming[way, d, h].astype(jnp.float32)).astype(jnp.bfloat16)

        @pl.when(d > 0)
        def _():
            p_copy(way, d, h).start()

        return carry

    lax.fori_loop(0, 4 * far, one_task, 0)

    for h in range(2):
        total = att[h]
        for way in q_ways(1, h):
            p_copy(way, 1, h).wait_recv()
            total = total + incoming[way, 0, h].astype(jnp.float32)
        inv = lax.rsqrt(jnp.mean(total * total, axis=0, keepdims=True) + norm_eps)
        normed = (total * inv).T * gates[h].astype(jnp.float32)
        hid[me_t, h] = normed.astype(jnp.bfloat16)
        y_send(hid, h, h_ss, h_rs)
    for j in range(1, n_tp):
        t = (me_t - j + n_tp) % n_tp
        rc(w_out_all.at[t], w_out_all.at[t], w_ss.at[j], w_rs.at[j], at_t(t)).wait_recv()
    y_forward(hid, 0, h_ss, h_rs)
    y_forward(hid, 1, h_ss, h_rs)
    w_all = jnp.concatenate([w_out_all[t] for t in range(n_tp)], axis=0)
    for h in range(2):
        y_wait(hid, h, h_ss, h_rs)
        rows = jnp.concatenate([hid[t, h] for t in range(n_tp)], axis=1)
        mixed = jnp.dot(rows, w_all, preferred_element_type=jnp.float32)
        out_ref[h] = (feats[me_t, h].astype(jnp.float32) + mixed).astype(jnp.bfloat16)
    for copy in sends:
        copy.wait_send()
    for d in range(1, far + 1):
        for h in range(2):
            for way in q_ways(d, h):
                p_copy(way, d, h).wait_send()


def per_device(
    nz, cand_feats, w_in, w_out, kv_cache, event_mask, block_counts, user_blocks, send_slots, cand_user
):
    rows = cand_feats.shape[0]
    half = rows // 2
    nx = lax.axis_size("user") // nz
    n_tp = lax.axis_size("tp")
    ny = n_tp // CORES
    far = nz // 2
    users, most = user_blocks.shape
    n_slots = nz * nx * CAP
    valid = jnp.arange(most, dtype=jnp.int32)[None, :] < block_counts[:, None]
    hit = (user_blocks[None] == jnp.arange(n_slots, dtype=jnp.int32)[:, None, None]) & valid[None]
    ext = jnp.where(jnp.any(hit, axis=2), 0.0, FAR).astype(jnp.float32)
    ext = jnp.pad(ext, ((0, 0), (0, DH - users))).reshape(nz, nx * CAP, DH)
    ext = jnp.pad(ext, ((0, 0), (0, 8 - nx * CAP), (0, 0)))
    who = cand_user.astype(jnp.float32).reshape(-1, DH)
    who = jnp.pad(who, ((0, 8 - who.shape[0]), (0, 0)))
    info = jnp.concatenate([jnp.broadcast_to(who[None], (nz, 8, DH)), ext], axis=1)

    bf16, f32 = jnp.bfloat16, jnp.float32
    dma = pltpu.SemaphoreType.DMA
    any_spec = pl.BlockSpec(memory_space=pl.ANY)
    vmem = pl.BlockSpec(memory_space=pltpu.VMEM)
    out = pl.pallas_call(
        functools.partial(kernel, (nz, nx, ny)),
        out_shape=jax.ShapeDtypeStruct((2, half, DH), bf16),
        in_specs=[pl.BlockSpec(memory_space=pltpu.SMEM), vmem, vmem] + [any_spec] * 4,
        out_specs=vmem,
        scratch_shapes=[
            pltpu.VMEM(kv_cache.shape, bf16),
            pltpu.VMEM((nz, nx, CAP, EVENTS, 2 * DH), bf16),
            pltpu.VMEM((nz, nx, CAP, EVENTS, 2 * DH), bf16),
            pltpu.VMEM((n_tp, 2, half, DH), bf16),
            pltpu.VMEM(w_in.shape, bf16),
            pltpu.VMEM(w_out.shape, bf16),
            pltpu.VMEM((n_tp, DH, DH), bf16),
            pltpu.VMEM((nz, 16, DH), f32),
            pltpu.VMEM((2 * far + 1, 2, DH, half), bf16),
            pltpu.VMEM((2, half, DH), bf16),
            pltpu.VMEM((DH, half), bf16),
            pltpu.VMEM((2, far, 2, DH, half), bf16),
            pltpu.VMEM((2, far, 2, DH, half), bf16),
            pltpu.VMEM((2, DH, half), f32),
            pltpu.VMEM((n_tp, 2, half, DH), bf16),
            dma((5,)),
            dma((nz, nx)),
            dma((nz, nx)),
            dma((nz,)),
            dma((nz,)),
            dma((2, 2 * ny - 1)),
            dma((2, 2 * ny - 1)),
            dma((2, 2 * ny - 1)),
            dma((2, 2 * ny - 1)),
            dma((n_tp,)),
            dma((n_tp,)),
            dma((2, far + 1, 2)),
            dma((2, far + 1, 2)),
            dma((2, far, 2)),
            dma((2, far, 2)),
        ],
        compiler_params=pltpu.CompilerParams(
            collective_id=0, has_side_effects=True, vmem_limit_bytes=52 * 2**20
        ),
        name="score",
    )(
        send_slots,
        info,
        event_mask.reshape(-1, 1, EVENTS),
        kv_cache,
        cand_feats.reshape(2, half, DH),
        w_in,
        w_out,
    )
    return out.reshape(rows, DH)


def solution(mesh):
    in_specs = (
        P("user", "tp"),
        P(None, "tp"),
        P("tp", None),
        P("user", None, "tp"),
        P("user", None),
        P("user"),
        P("user", None),
        P("user", None),
        P("user"),
    )
    return jax.shard_map(
        functools.partial(per_device, Z_SIZE),
        mesh=mesh,
        in_specs=in_specs,
        out_specs=P("user", "tp"),
        check_vma=False,
    )
```

```python
import functools

import jax
import jax.numpy as jnp
from jax import lax
from jax.experimental import pallas as pl
from jax.experimental.pallas import tpu as pltpu
from jax.sharding import PartitionSpec as P

DH = 128
EVENTS = 128
CAP = 2
CORES = 2
Z_SIZE = 8
CHUNKS = 4
WINDOW = 3
norm_eps = 1e-06
FAR = -float(2**30)
HALF_SCALE = 0.5 * DH**-0.5
MESH = pl.DeviceIdType.MESH


def silu(v):
    x = 0.5 * v
    return x + x * jnp.tanh(x)


def kernel(
    dims,
    slots_ref,
    counts_ref,
    blocks_ref,
    who_hbm,
    mask_hbm,
    kv_hbm,
    feats_hbm,
    w_in_hbm,
    w_out_hbm,
    out_ref,
    who_v,
    mask_v,
    kv_v,
    snd,
    kvr,
    feats,
    w_in_v,
    w_out_v,
    w_out_all,
    ext_v,
    info_out,
    info_all,
    qs,
    gates,
    onehot,
    parts,
    incoming,
    hid,
    loc_sem,
    x_ss,
    x_rs,
    info_ss,
    info_rs,
    f_ss,
    f_rs,
    h_ss,
    h_rs,
    w_ss,
    w_rs,
    q_ss,
    q_rs,
    p_ss,
    p_rs,
):
    nz, nx, ny = dims
    far = nz // 2
    win = WINDOW
    rows = feats.shape[2]
    n_tp = ny * CORES
    n_blk = nx * CAP
    users, most = blocks_ref.shape
    me_u = lax.axis_index("user")
    me_t = lax.axis_index("tp")
    z, x = me_u // nx, me_u % nx
    y, core = me_t // CORES, me_t % CORES

    def at_z(d):
        return ((z + d + nz) % nz * nx + x, me_t)

    def at_x(j):
        return (z * nx + (x + j) % nx, me_t)

    def at_t(t):
        return (me_u, t)

    def rc(src, dst, ss, rs, dev):
        return pltpu.make_async_remote_copy(
            src_ref=src, dst_ref=dst, send_sem=ss, recv_sem=rs,
            device_id=dev, device_id_type=MESH,
        )

    f_load = pltpu.make_async_copy(feats_hbm, feats.at[me_t], loc_sem.at[0])
    kv_load = pltpu.make_async_copy(kv_hbm, kv_v, loc_sem.at[1])
    wi_load = pltpu.make_async_copy(w_in_hbm, w_in_v, loc_sem.at[2])
    wo_load = pltpu.make_async_copy(w_out_hbm, w_out_v, loc_sem.at[3])
    mask_load = pltpu.make_async_copy(mask_hbm, mask_v, loc_sem.at[4])
    who_load = pltpu.make_async_copy(who_hbm, who_v, loc_sem.at[5])
    for load in (f_load, who_load, mask_load, kv_load, wi_load, wo_load):
        load.start()

    barrier = pltpu.get_barrier_semaphore()
    peers = [at_t((me_t + j) % n_tp) for j in range(1, n_tp)]
    peers += [at_x(j) for j in range(1, nx)]
    peers += [at_z(d * w) for d in range(1, win + 1) for w in (1, -1)]
    peers += [
        ((z + d * w + nz) % nz * nx + (x + j) % nx, me_t)
        for d in range(1, far - win + 1) for w in (1, -1) for j in range(1, nx)
    ]
    for dev in peers:
        pl.semaphore_signal(barrier, inc=1, device_id=dev, device_id_type=MESH)

    onehot[...] = jnp.zeros_like(onehot)
    shape = (nz * n_blk, DH)
    slot_id = lax.broadcasted_iota(jnp.int32, shape, 0)
    lane = lax.broadcasted_iota(jnp.int32, shape, 1)
    ext = jnp.where(lane < users, FAR, 0.0)
    for u in range(users):
        hit = jnp.zeros(shape, jnp.bool_)
        for j in range(most):
            held = jnp.where(j < counts_ref[u], blocks_ref[u, j], -1)
            hit = jnp.logical_or(hit, slot_id == held)
        ext = jnp.where(jnp.logical_and(hit, lane == u), 0.0, ext)
    ext_v[...] = ext
    who_load.wait()
    who = who_v[...].astype(jnp.float32)

    def tables(ref, i, way, d):
        ref[i, 0 : who.shape[0]] = who
        for g in range(far - win + 1 if d == win else 1):
            holder = (z + (d + g) * (1 - 2 * way) + nz) % nz
            ref[i, 8 + 8 * g : 8 + 8 * g + n_blk] = ext_v[pl.ds(pl.multiple_of(holder * n_blk, n_blk), n_blk)]

    tables(info_all, 0, 0, 0)
    for way in range(2):
        for d in range(1, win + 1):
            tables(info_out, way * win + d, way, d)
    pl.semaphore_wait(barrier, len(peers))

    sends = []

    def go(copy):
        copy.start()
        sends.append(copy)

    partner = y * CORES + 1 - core

    def y_src(j, c):
        return (y - j + ny) % ny * CORES + c

    def y_sends(buf, c, ss, rs):
        own = buf.at[me_t, c]
        devs = [at_t(partner)] + [at_t((y + j) % ny * CORES + core) for j in range(1, ny)]
        return [rc(own, own, ss.at[c, j], rs.at[c, j], dev) for j, dev in enumerate(devs)]

    def y_passed(buf, c, ss, rs, j, side):
        got = buf.at[y_src(j, side), c]
        k = ny - 1 + j if j else 0
        return rc(got, got, ss.at[c, k], rs.at[c, k], at_t(partner))

    def y_forward(buf, c, ss, rs):
        for j in range(1, ny):
            got = buf.at[y_src(j, core), c]
            rc(got, got, ss.at[c, j], rs.at[c, j], at_t(partner)).wait_recv()
            y_passed(buf, c, ss, rs, j, core).start()

    def y_wait(buf, c, ss, rs):
        for j in range(ny):
            y_passed(buf, c, ss, rs, j, 1 - core).wait_recv()

    def y_drain(buf, c, ss, rs):
        for copy in y_sends(buf, c, ss, rs):
            copy.wait_send()
        for j in range(1, ny):
            y_passed(buf, c, ss, rs, j, core).wait_send()

    f_load.wait()
    for c in range(CHUNKS):
        for copy in y_sends(feats, c, f_ss, f_rs):
            copy.start()

    def info_copy(i, dev):
        return rc(info_out.at[i], info_all.at[i], info_ss.at[i], info_rs.at[i], dev)

    for way in range(2):
        for d in range(1, win + 1):
            go(info_copy(way * win + d, at_z(d * (1 - 2 * way))))

    def unit(way, d):
        return jnp.maximum(2 * d - 1 + way, 0) if not isinstance(d, int) else (2 * d - 1 + way if d else 0)

    def x_copy(u, j):
        return rc(snd.at[u, j], kvr.at[u, j], x_ss.at[u, j], x_rs.at[u, j], at_x(j))

    def hop_copy(way, d, j):
        u = unit(way, d)
        dev = ((z - (d - win) * (1 - 2 * way) + nz) % nz * nx + (x + j) % nx, me_t)
        if d < far:
            return rc(snd.at[u, j], kvr.at[u, j], x_ss.at[u, j], x_rs.at[u, j], dev)
        return rc(
            snd.at[2 * far - 1, j, way], kvr.at[u, j, way], x_ss.at[u, j], x_rs.at[u, j], dev
        )

    def prepare(n):
        way, d = (n + 1) % 2, far - (n + 1) // 2
        if isinstance(n, int) and d == far:
            way = 0
        u = unit(way, d)
        ranker = (z - d * (1 - 2 * way) + nz) % nz * nx

        def one(i, carry):
            j, c = i // CAP, i % CAP
            slot = slots_ref[c, ranker + (x + j) % nx]
            block = kv_v[slot]
            live = mask_v[slot].astype(jnp.float32).astype(jnp.bfloat16)
            snd[u, j, c, :, 0:DH] = block[:, 0:DH]
            snd[u, j, c, :, DH:] = block[:, DH:].T * live
            return carry

        lax.fori_loop(0, n_blk, one, 0)
        if isinstance(n, int) and d > win:
            for j in range(nx):
                for w in range(2) if d == far else (way,):
                    hop_copy(w, d, j).start()
        else:
            for j in range(1, nx):
                x_copy(u, j).start()

    def q_copy(way, d, c):
        before = 0 if d == 1 else way * win + d - 1
        return rc(
            qs.at[before, c], qs.at[way * win + d, c],
            q_ss.at[way, d, c], q_rs.at[way, d, c], at_z(1 - 2 * way),
        )

    def p_copy(way, d, c):
        return rc(
            parts.at[way, d - 1, c], incoming.at[way, d - 1, c],
            p_ss.at[way, d - 1, c], p_rs.at[way, d - 1, c], at_z(2 * way - 1),
        )

    def project(c):
        block = jnp.concatenate([feats[t, c] for t in range(n_tp)], axis=1)
        act = silu(jnp.dot(block, w_in_v[...], preferred_element_type=jnp.float32))
        qs[0, c] = act[:, 0:DH].T.astype(jnp.bfloat16)
        gates[c] = act[:, DH:].astype(jnp.bfloat16)

    def attend(i, c, blocks):
        user = lax.broadcasted_iota(jnp.int32, (16, DH), 0).astype(jnp.float32)
        per = rows // DH
        for r in range(per):
            row = info_all[i, pl.ds(c * per + r, 1), :]
            onehot[0:16, r * DH : (r + 1) * DH] = jnp.where(row == user, 1.0, 0.0).astype(jnp.bfloat16)
        keys, values = [], []
        for block, b in blocks:
            row = info_all[i, pl.ds(8 + b, 1), :].astype(jnp.bfloat16)
            keys.append(jnp.concatenate([block[:, 0:DH], jnp.broadcast_to(row, (EVENTS, DH))], axis=1))
            values.append(block[:, DH:])
        rhs = jnp.concatenate([qs[i, c], onehot[...]], axis=0)
        v = HALF_SCALE * jnp.dot(
            jnp.concatenate(keys, axis=0), rhs, preferred_element_type=jnp.float32
        )
        w = (v + v * jnp.tanh(v)).astype(jnp.bfloat16)
        return jnp.dot(jnp.concatenate(values, axis=1), w, preferred_element_type=jnp.float32)

    def entry(j, s):
        return (x - j + nx) % nx * CAP + s

    def near_blocks(u):
        return [
            (snd[u, 0, s] if j == 0 else kvr[u, j, s], entry(j, s)) for j in range(nx) for s in range(CAP)
        ]

    def edge_blocks(way):
        blocks = near_blocks(unit(way, win))
        for d in range(win + 1, far + 1):
            u = 2 * d - 1 + way
            for j in range(nx):
                if d < far:
                    blocks += [(kvr[u, j, s], 8 * (d - win) + entry(j, s)) for s in range(CAP)]
                else:
                    blocks += [(kvr[u, j, way], 8 * (d - win) + entry(j, way))]
        return blocks

    def in_range(c):
        return jnp.logical_and(c >= 0, c < CHUNKS)

    def tick(t, carry):
        @pl.when(t < CHUNKS)
        def _():
            y_wait(feats, t, f_ss, f_rs)
            project(t)
            for way in range(2):
                q_copy(way, 1, t).start()

        @pl.when(t + 1 < CHUNKS)
        def _():
            y_forward(feats, t + 1, f_ss, f_rs)

        for d in range(win - 1, 0, -1):
            c = t - d

            @pl.when(in_range(c))
            def _():
                for way in range(2):
                    q_copy(way, d, c).wait_recv()
                    q_copy(way, d + 1, c).start()

        @pl.when(t + 3 < nz)
        def _():
            prepare(t + 3)

        c = t - win

        @pl.when(in_range(c))
        def _():
            def edge(way, carry):
                i = way * win + win

                @pl.when(c == 0)
                def _():
                    for j in range(1, nx):
                        x_copy(unit(way, win), j).wait_recv()
                    for d in range(win + 1, far + 1):
                        for j in range(nx):
                            got = kvr.at[2 * d - 1 + way, j]
                            if d == far:
                                got = got.at[way]
                            sems = x_ss.at[2 * d - 1 + way, j], x_rs.at[2 * d - 1 + way, j]
                            rc(got, got, *sems, at_x(1)).wait_recv()
                    info_copy(i, at_z(1)).wait_recv()

                q_copy(way, win, c).wait_recv()
                parts[way, win - 1, c] = attend(i, c, edge_blocks(way)).astype(jnp.bfloat16)
                p_copy(way, win, c).start()
                return carry

            lax.fori_loop(0, 2, edge, 0)

        return carry

    def inner(m, carry):
        d, c, way = win - 1 - m // (2 * CHUNKS), m // 2 % CHUNKS, m % 2
        u, i = 2 * d - 1 + way, way * win + d

        @pl.when(c == 0)
        def _():
            for j in range(1, nx):
                x_copy(u, j).wait_recv()
            info_copy(i, at_z(1)).wait_recv()

        total = attend(i, c, near_blocks(u))
        p_copy(way, d + 1, c).wait_recv()
        got = incoming[way, d, c].astype(jnp.float32)
        parts[way, d - 1, c] = (total + got).astype(jnp.bfloat16)
        p_copy(way, d, c).start()
        return carry

    def finish(c, carry):
        total = attend(0, c, near_blocks(0))
        for way in range(2):
            p_copy(way, 1, c).wait_recv()
            total = total + incoming[way, 0, c].astype(jnp.float32)
        inv = lax.rsqrt(jnp.mean(total * total, axis=0, keepdims=True) + norm_eps)
        normed = (total * inv).T * gates[c].astype(jnp.float32)
        hid[me_t, c] = normed.astype(jnp.bfloat16)
        for copy in y_sends(hid, c, h_ss, h_rs):
            copy.start()
        return carry

    def output(t, carry):
        @pl.when(t < CHUNKS)
        def _():
            y_forward(hid, t, h_ss, h_rs)

        @pl.when(t > 0)
        def _():
            c = t - 1
            y_wait(hid, c, h_ss, h_rs)
            block = jnp.concatenate([hid[s, c] for s in range(n_tp)], axis=1)
            w_all = jnp.concatenate([w_out_all[s] for s in range(n_tp)], axis=0)
            mixed = jnp.dot(block, w_all, preferred_element_type=jnp.float32)
            out_ref[c] = (feats[me_t, c].astype(jnp.float32) + mixed).astype(jnp.bfloat16)

        return carry

    mask_load.wait()
    kv_load.wait()
    prepare(0)
    wi_load.wait()
    wo_load.wait()
    w_out_all[me_t] = w_out_v[:, pl.ds(pl.multiple_of(me_t * DH, DH), DH)]
    for j in range(1, n_tp):
        s = (me_t + j) % n_tp
        cols = pl.ds(pl.multiple_of(s * DH, DH), DH)
        go(rc(w_out_v.at[:, cols], w_out_all.at[me_t], w_ss.at[j], w_rs.at[j], at_t(s)))
    prepare(1)
    y_forward(feats, 0, f_ss, f_rs)
    prepare(2)
    lax.fori_loop(0, CHUNKS + win, tick, 0)
    lax.fori_loop(0, 2 * CHUNKS * (win - 1), inner, 0)
    for j in range(1, nx):
        x_copy(0, j).wait_recv()
    lax.fori_loop(0, CHUNKS, finish, 0)
    for j in range(1, n_tp):
        s = (me_t - j + n_tp) % n_tp
        rc(w_out_all.at[s], w_out_all.at[s], w_ss.at[j], w_rs.at[j], at_t(s)).wait_recv()
    lax.fori_loop(0, CHUNKS + 1, output, 0)

    for copy in sends:
        copy.wait_send()

    def drain(c, carry):
        y_drain(feats, c, f_ss, f_rs)
        y_drain(hid, c, h_ss, h_rs)
        for way in range(2):
            for d in range(1, win + 1):
                q_copy(way, d, c).wait_send()
                p_copy(way, d, c).wait_send()
        return carry

    lax.fori_loop(0, CHUNKS, drain, 0)
    for way in range(2):
        for d in range(win + 1, far + 1):
            for j in range(nx):
                hop_copy(way, d, j).wait_send()

    def drain_x(u, carry):
        for j in range(1, nx):
            x_copy(u, j).wait_send()
        return carry

    lax.fori_loop(0, 2 * win + 1, drain_x, 0)


def per_device(
    nz, cand_feats, w_in, w_out, kv_cache, event_mask, block_counts, user_blocks, send_slots, cand_user
):
    n_rows = cand_feats.shape[0]
    rows = n_rows // CHUNKS
    nx = lax.axis_size("user") // nz
    n_tp = lax.axis_size("tp")
    ny = n_tp // CORES
    far = nz // 2
    win = WINDOW
    units = 2 * far + 1
    tab = 8 * (far - win + 2)

    bf16, f32 = jnp.bfloat16, jnp.float32
    dma = pltpu.SemaphoreType.DMA
    hbm = pl.BlockSpec(memory_space=pltpu.HBM)
    smem = pl.BlockSpec(memory_space=pltpu.SMEM)
    mask = event_mask.reshape(-1, 1, EVENTS)
    who = cand_user.reshape(-1, DH)
    out = pl.pallas_call(
        functools.partial(kernel, (nz, nx, ny)),
        out_shape=jax.ShapeDtypeStruct((CHUNKS, rows, DH), bf16),
        in_specs=[smem] * 3 + [hbm] * 6,
        out_specs=pl.BlockSpec(memory_space=pltpu.VMEM),
        scratch_shapes=[
            pltpu.VMEM(who.shape, jnp.int32),
            pltpu.VMEM(mask.shape, jnp.int32),
            pltpu.VMEM(kv_cache.shape, bf16),
            pltpu.VMEM((units, nx, CAP, EVENTS, 2 * DH), bf16),
            pltpu.VMEM((units, nx, CAP, EVENTS, 2 * DH), bf16),
            pltpu.VMEM((n_tp, CHUNKS, rows, DH), bf16),
            pltpu.VMEM(w_in.shape, bf16),
            pltpu.VMEM(w_out.shape, bf16),
            pltpu.VMEM((n_tp, DH, DH), bf16),
            pltpu.VMEM((nz * nx * CAP, DH), f32),
            pltpu.VMEM((2 * win + 1, tab, DH), f32),
            pltpu.VMEM((2 * win + 1, tab, DH), f32),
            pltpu.VMEM((2 * win + 1, CHUNKS, DH, rows), bf16),
            pltpu.VMEM((CHUNKS, rows, DH), bf16),
            pltpu.VMEM((DH, rows), bf16),
            pltpu.VMEM((2, win, CHUNKS, DH, rows), bf16),
            pltpu.VMEM((2, win, CHUNKS, DH, rows), bf16),
            pltpu.VMEM((n_tp, CHUNKS, rows, DH), bf16),
            dma((6,)),
            dma((units, nx)),
            dma((units, nx)),
            dma((2 * win + 1,)),
            dma((2 * win + 1,)),
            dma((CHUNKS, 2 * ny - 1)),
            dma((CHUNKS, 2 * ny - 1)),
            dma((CHUNKS, 2 * ny - 1)),
            dma((CHUNKS, 2 * ny - 1)),
            dma((n_tp,)),
            dma((n_tp,)),
            dma((2, win + 1, CHUNKS)),
            dma((2, win + 1, CHUNKS)),
            dma((2, win, CHUNKS)),
            dma((2, win, CHUNKS)),
        ],
        compiler_params=pltpu.CompilerParams(
            collective_id=0, has_side_effects=True, vmem_limit_bytes=60 * 2**20
        ),
        name="score",
    )(
        send_slots.T,
        block_counts,
        user_blocks,
        who,
        mask,
        kv_cache,
        cand_feats.reshape(CHUNKS, rows, DH),
        w_in,
        w_out,
    )
    return out.reshape(n_rows, DH)


def solution(mesh):
    in_specs = (
        P("user", "tp"),
        P(None, "tp"),
        P("tp", None),
        P("user", None, "tp"),
        P("user", None),
        P("user"),
        P("user", None),
        P("user", None),
        P("user"),
    )
    return jax.shard_map(
        functools.partial(per_device, Z_SIZE),
        mesh=mesh,
        in_specs=in_specs,
        out_specs=P("user", "tp"),
        check_vma=False,
    )
```

```python
import functools

import jax
import jax.numpy as jnp
from jax import lax
from jax.experimental import pallas as pl
from jax.experimental.pallas import tpu as pltpu
from jax.sharding import PartitionSpec as P

DH = 128
EVENTS = 128
CAP = 2
CORES = 2
Z_SIZE = 8
CHUNKS = 4
WINDOW = 3
norm_eps = 1e-06
FAR = -float(2**30)
HALF_SCALE = 0.5 * DH**-0.5
MESH = pl.DeviceIdType.MESH


def silu(v):
    x = 0.5 * v
    return x + x * jnp.tanh(x)


def kernel(
    dims,
    slots_ref,
    counts_ref,
    blocks_ref,
    who_hbm,
    mask_hbm,
    kv_hbm,
    feats_hbm,
    w_in_hbm,
    w_out_hbm,
    out_ref,
    who_v,
    mask_v,
    kv_v,
    snd,
    kvr,
    feats,
    w_in_v,
    w_out_v,
    w_out_all,
    ext_v,
    info_out,
    info_all,
    qs,
    gates,
    onehot,
    parts,
    incoming,
    hid,
    loc_sem,
    x_ss,
    x_rs,
    info_ss,
    info_rs,
    f_ss,
    f_rs,
    h_ss,
    h_rs,
    w_ss,
    w_rs,
    q_ss,
    q_rs,
    p_ss,
    p_rs,
):
    nz, nx, ny = dims
    far = nz // 2
    win = WINDOW
    rows = feats.shape[2]
    n_tp = ny * CORES
    n_blk = nx * CAP
    users, most = blocks_ref.shape
    me_u = lax.axis_index("user")
    me_t = lax.axis_index("tp")
    z, x = me_u // nx, me_u % nx
    y, core = me_t // CORES, me_t % CORES

    z_to = {d: ((z + d + nz) % nz * nx + x, me_t) for d in range(-win, win + 1)}
    x_to = [(z * nx + (x + j) % nx, me_t) for j in range(nx)]
    zx_to = {
        (d, j): ((z + d + nz) % nz * nx + (x + j) % nx, me_t)
        for d in range(win - far, far - win + 1) if d for j in range(nx)
    }
    partner = y * CORES + 1 - core
    y_to = [(me_u, partner)] + [(me_u, (y + j) % ny * CORES + core) for j in range(1, ny)]
    y_own = [(y - j + ny) % ny * CORES + core for j in range(ny)]
    y_other = [(y - j + ny) % ny * CORES + 1 - core for j in range(ny)]
    entries = [(x - j + nx) % nx * CAP for j in range(nx)]

    def at_z(d):
        return z_to[d]

    def at_x(j):
        return x_to[j]

    def at_t(t):
        return (me_u, t)

    def rc(src, dst, ss, rs, dev):
        return pltpu.make_async_remote_copy(
            src_ref=src, dst_ref=dst, send_sem=ss, recv_sem=rs,
            device_id=dev, device_id_type=MESH,
        )

    barrier = pltpu.get_barrier_semaphore()
    peers = [at_t((me_t + j) % n_tp) for j in range(1, n_tp)]
    peers += [at_x(j) for j in range(1, nx)]
    peers += [at_z(d * w) for d in range(1, win + 1) for w in (1, -1)]
    peers += [
        ((z + d * w + nz) % nz * nx + (x + j) % nx, me_t)
        for d in range(1, far - win + 1) for w in (1, -1) for j in range(1, nx)
    ]
    for dev in peers:
        pl.semaphore_signal(barrier, inc=1, device_id=dev, device_id_type=MESH)

    f_load = pltpu.make_async_copy(feats_hbm, feats.at[me_t], loc_sem.at[0])
    kv_step = kv_v.shape[0] // 8
    kv_loads = [
        pltpu.make_async_copy(kv_hbm.at[pl.ds(i * kv_step, kv_step)], kv_v.at[pl.ds(i * kv_step, kv_step)], loc_sem.at[6 + i])
        for i in range(8)
    ]
    wi_load = pltpu.make_async_copy(w_in_hbm, w_in_v, loc_sem.at[2])
    wo_load = pltpu.make_async_copy(w_out_hbm, w_out_v, loc_sem.at[3])
    mask_load = pltpu.make_async_copy(mask_hbm, mask_v, loc_sem.at[4])
    who_load = pltpu.make_async_copy(who_hbm, who_v, loc_sem.at[5])
    for load in [f_load, mask_load, *kv_loads, who_load, wi_load, wo_load]:
        load.start()

    onehot[...] = jnp.zeros_like(onehot)
    shape = (nz * n_blk, DH)
    slot_id = lax.broadcasted_iota(jnp.int32, shape, 0)
    lane = lax.broadcasted_iota(jnp.int32, shape, 1)
    ext = jnp.where(lane < users, FAR, 0.0)
    for u in range(users):
        hit = jnp.zeros(shape, jnp.bool_)
        for j in range(most):
            held = jnp.where(j < counts_ref[u], blocks_ref[u, j], -1)
            hit = jnp.logical_or(hit, slot_id == held)
        ext = jnp.where(jnp.logical_and(hit, lane == u), 0.0, ext)
    ext_v[...] = ext
    who_load.wait()
    who = who_v[...].astype(jnp.float32)

    def tables(ref, i, way, d):
        ref[i, 0 : who.shape[0]] = who
        for g in range(far - win + 1 if d == win else 1):
            holder = (z + (d + g) * (1 - 2 * way) + nz) % nz
            ref[i, 8 + 8 * g : 8 + 8 * g + n_blk] = ext_v[pl.ds(pl.multiple_of(holder * n_blk, n_blk), n_blk)]

    tables(info_all, 0, 0, 0)
    for way in range(2):
        for d in range(1, win + 1):
            tables(info_out, way * win + d, way, d)
    pl.semaphore_wait(barrier, len(peers))

    sends = []

    def go(copy):
        copy.start()
        sends.append(copy)

    def y_sends(buf, c, ss, rs, src=None):
        own = buf.at[me_t, c]
        src = own if src is None else src
        devs = y_to
        return [rc(src, own, ss.at[c, j], rs.at[c, j], dev) for j, dev in enumerate(devs)]

    def y_passed(buf, c, ss, rs, j, srcs):
        got = buf.at[srcs[j], c]
        k = ny - 1 + j if j else 0
        return rc(got, got, ss.at[c, k], rs.at[c, k], at_t(partner))

    def y_forward(buf, c, ss, rs):
        for j in range(1, ny):
            got = buf.at[y_own[j], c]
            rc(got, got, ss.at[c, j], rs.at[c, j], at_t(partner)).wait_recv()
            y_passed(buf, c, ss, rs, j, y_own).start()

    def y_wait(buf, c, ss, rs):
        for j in range(ny):
            y_passed(buf, c, ss, rs, j, y_other).wait_recv()

    def y_drain(buf, c, ss, rs):
        for copy in y_sends(buf, c, ss, rs):
            copy.wait_send()
        for j in range(1, ny):
            y_passed(buf, c, ss, rs, j, y_own).wait_send()

    for c in range(CHUNKS):
        for copy in y_sends(feats, c, f_ss, f_rs, feats_hbm.at[c]):
            copy.start()
    f_load.wait()

    def info_copy(i, dev):
        return rc(info_out.at[i], info_all.at[i], info_ss.at[i], info_rs.at[i], dev)

    for way in range(2):
        for d in range(1, win + 1):
            go(info_copy(way * win + d, at_z(d * (1 - 2 * way))))

    def unit(way, d):
        return jnp.maximum(2 * d - 1 + way, 0) if not isinstance(d, int) else (2 * d - 1 + way if d else 0)

    def x_copy(u, j):
        return rc(snd.at[u, j], kvr.at[u, j], x_ss.at[u, j], x_rs.at[u, j], at_x(j))

    def hop_copy(way, d, j):
        u = unit(way, d)
        dev = zx_to[(win - d) * (1 - 2 * way), j]
        if d < far:
            return rc(snd.at[u, j], kvr.at[u, j], x_ss.at[u, j], x_rs.at[u, j], dev)
        return rc(
            snd.at[2 * far - 1, j, way], kvr.at[u, j, way], x_ss.at[u, j], x_rs.at[u, j], dev
        )

    def prepare(n):
        way, d = (n + 1) % 2, far - (n + 1) // 2
        if isinstance(n, int) and d == far:
            way = 0
        u = unit(way, d)
        ranker = (z - d * (1 - 2 * way) + nz) % nz * nx

        def one(i, carry):
            j, c = i // CAP, i % CAP
            slot = slots_ref[c, ranker + (x + j) % nx]
            block = kv_v[slot]
            live = mask_v[slot].astype(jnp.float32).astype(jnp.bfloat16)
            snd[u, j, c, :, 0:DH] = block[:, 0:DH]
            snd[u, j, c, :, DH:] = block[:, DH:].T * live
            return carry

        lax.fori_loop(0, n_blk, one, 0, unroll=4)
        if isinstance(n, int) and d > win:
            for j in range(nx):
                for w in range(2) if d == far else (way,):
                    hop_copy(w, d, j).start()
        else:
            for j in range(1, nx):
                x_copy(u, j).start()

    def q_copy(way, d, c):
        before = 0 if d == 1 else way * win + d - 1
        return rc(
            qs.at[before, c], qs.at[way * win + d, c],
            q_ss.at[way, d, c], q_rs.at[way, d, c], z_to[1 - 2 * way if isinstance(way, int) else 1],
        )

    def inward(way):
        if isinstance(way, int):
            return z_to[2 * way - 1]
        return (jnp.where(way == 0, z_to[-1][0], z_to[1][0]), me_t)

    def p_copy(way, d, c):
        return rc(
            parts.at[way, d - 1, c], incoming.at[way, d - 1, c],
            p_ss.at[way, d - 1, c], p_rs.at[way, d - 1, c], inward(way),
        )

    def project(c):
        block = jnp.concatenate([feats[t, c] for t in range(n_tp)], axis=1)
        act = silu(jnp.dot(block, w_in_v[...], preferred_element_type=jnp.float32))
        qs[0, c] = act[:, 0:DH].T.astype(jnp.bfloat16)
        gates[c] = act[:, DH:].astype(jnp.bfloat16)

    def attend(i, c, blocks):
        user = lax.broadcasted_iota(jnp.int32, (16, DH), 0).astype(jnp.float32)
        per = rows // DH
        for r in range(per):
            row = info_all[i, pl.ds(c * per + r, 1), :]
            onehot[0:16, r * DH : (r + 1) * DH] = jnp.where(row == user, 1.0, 0.0).astype(jnp.bfloat16)
        keys, values = [], []
        for block, b in blocks:
            row = info_all[i, pl.ds(8 + b, 1), :].astype(jnp.bfloat16)
            keys.append(jnp.concatenate([block[:, 0:DH], jnp.broadcast_to(row, (EVENTS, DH))], axis=1))
            values.append(block[:, DH:])
        rhs = jnp.concatenate([qs[i, c], onehot[...]], axis=0)
        v = HALF_SCALE * jnp.dot(
            jnp.concatenate(keys, axis=0), rhs, preferred_element_type=jnp.float32
        )
        w = (v + v * jnp.tanh(v)).astype(jnp.bfloat16)
        return jnp.dot(jnp.concatenate(values, axis=1), w, preferred_element_type=jnp.float32)

    def entry(j, s):
        return entries[j] + s

    def near_blocks(u):
        return [
            (snd[u, 0, s] if j == 0 else kvr[u, j, s], entry(j, s)) for j in range(nx) for s in range(CAP)
        ]

    def edge_blocks(way):
        blocks = near_blocks(unit(way, win))
        for d in range(win + 1, far + 1):
            u = 2 * d - 1 + way
            for j in range(nx):
                if d < far:
                    blocks += [(kvr[u, j, s], 8 * (d - win) + entry(j, s)) for s in range(CAP)]
                else:
                    blocks += [(kvr[u, j, way], 8 * (d - win) + entry(j, way))]
        return blocks

    def in_range(c):
        return jnp.logical_and(c >= 0, c < CHUNKS)

    def tick(t, carry):
        @pl.when(t < CHUNKS)
        def _():
            y_wait(feats, t, f_ss, f_rs)
            project(t)
            for way in range(2):
                q_copy(way, 1, t).start()

        @pl.when(t + 1 < CHUNKS)
        def _():
            y_forward(feats, t + 1, f_ss, f_rs)

        for d in range(win - 1, 0, -1):
            c = t - d

            @pl.when(in_range(c))
            def _():
                for way in range(2):
                    q_copy(way, d, c).wait_recv()
                    q_copy(way, d + 1, c).start()

        c = t - win

        @pl.when(in_range(c))
        def _():
            def edge(way, carry):
                i = way * win + win

                @pl.when(c == 0)
                def _():
                    for j in range(1, nx):
                        x_copy(unit(way, win), j).wait_recv()
                    for d in range(win + 1, far + 1):
                        for j in range(nx):
                            got = kvr.at[2 * d - 1 + way, j]
                            if d == far:
                                got = got.at[way]
                            sems = x_ss.at[2 * d - 1 + way, j], x_rs.at[2 * d - 1 + way, j]
                            rc(got, got, *sems, at_x(1)).wait_recv()
                    info_copy(i, at_z(1)).wait_recv()

                q_copy(way, win, c).wait_recv()
                parts[way, win - 1, c] = attend(i, c, edge_blocks(way)).astype(jnp.bfloat16)
                p_copy(way, win, c).start()
                return carry

            lax.fori_loop(0, 2, edge, 0)

        return carry

    def inner(m, carry):
        d, c, way = win - 1 - m // (2 * CHUNKS), (m >> 1) & (CHUNKS - 1), m & 1
        u, i = 2 * d - 1 + way, way * win + d

        @pl.when(c == 0)
        def _():
            for j in range(1, nx):
                x_copy(u, j).wait_recv()
            info_copy(i, at_z(1)).wait_recv()

        total = attend(i, c, near_blocks(u))
        p_copy(way, d + 1, c).wait_recv()
        got = incoming[way, d, c].astype(jnp.float32)
        parts[way, d - 1, c] = (total + got).astype(jnp.bfloat16)
        p_copy(way, d, c).start()
        return carry

    def finish(c, carry):
        total = attend(0, c, near_blocks(0))
        for way in range(2):
            p_copy(way, 1, c).wait_recv()
            total = total + incoming[way, 0, c].astype(jnp.float32)
        inv = lax.rsqrt(jnp.mean(total * total, axis=0, keepdims=True) + norm_eps)
        normed = (total * inv).T * gates[c].astype(jnp.float32)
        hid[me_t, c] = normed.astype(jnp.bfloat16)
        for copy in y_sends(hid, c, h_ss, h_rs):
            copy.start()
        return carry

    def output(t, carry):
        @pl.when(t < CHUNKS)
        def _():
            y_forward(hid, t, h_ss, h_rs)
            for copy in y_sends(hid, t, h_ss, h_rs):
                copy.wait_send()
            for way in range(2):
                for d in range(1, win + 1):
                    p_copy(way, d, t).wait_send()

        @pl.when(t > 0)
        def _():
            c = t - 1
            y_wait(hid, c, h_ss, h_rs)
            block = jnp.concatenate([hid[s, c] for s in range(n_tp)], axis=1)
            w_all = jnp.concatenate([w_out_all[s] for s in range(n_tp)], axis=0)
            mixed = jnp.dot(block, w_all, preferred_element_type=jnp.float32)
            out_ref[c] = (feats[me_t, c].astype(jnp.float32) + mixed).astype(jnp.bfloat16)
            for j in range(1, ny):
                y_passed(hid, c, h_ss, h_rs, j, y_own).wait_send()

        return carry

    mask_load.wait()
    for load in kv_loads:
        load.wait()
    prepare(0)
    prepare(1)
    prepare(2)
    lax.fori_loop(3, 8, lambda n, carry: (prepare(n), carry)[1], 0)
    y_forward(feats, 0, f_ss, f_rs)
    wi_load.wait()
    wo_load.wait()
    w_out_all[me_t] = w_out_v[:, pl.ds(pl.multiple_of(me_t * DH, DH), DH)]
    for j in range(1, n_tp):
        s = (me_t + j) % n_tp
        cols = pl.ds(pl.multiple_of(s * DH, DH), DH)
        go(rc(w_out_v.at[:, cols], w_out_all.at[me_t], w_ss.at[j], w_rs.at[j], at_t(s)))
    lax.fori_loop(0, CHUNKS + win, tick, 0)
    lax.fori_loop(0, 2 * CHUNKS * (win - 1), inner, 0)
    for copy in sends:
        copy.wait_send()

    def drain_early(c, carry):
        y_drain(feats, c, f_ss, f_rs)
        for way in range(2):
            for d in range(1, win + 1):
                q_copy(way, d, c).wait_send()
        return carry

    lax.fori_loop(0, CHUNKS, drain_early, 0)
    for way in range(2):
        for d in range(win + 1, far + 1):
            for j in range(nx):
                hop_copy(way, d, j).wait_send()

    def drain_x(u, carry):
        for j in range(1, nx):
            x_copy(u, j).wait_send()
        return carry

    lax.fori_loop(1, 2 * win + 1, drain_x, 0)
    for j in range(1, n_tp):
        s = (me_t - j + n_tp) % n_tp
        rc(w_out_all.at[s], w_out_all.at[s], w_ss.at[j], w_rs.at[j], at_t(s)).wait_recv()
    for j in range(1, nx):
        x_copy(0, j).wait_recv()
    lax.fori_loop(0, CHUNKS, finish, 0)
    for j in range(1, nx):
        x_copy(0, j).wait_send()
    lax.fori_loop(0, CHUNKS + 1, output, 0)


def per_device(
    nz, cand_feats, w_in, w_out, kv_cache, event_mask, block_counts, user_blocks, send_slots, cand_user
):
    n_rows = cand_feats.shape[0]
    rows = n_rows // CHUNKS
    nx = lax.axis_size("user") // nz
    n_tp = lax.axis_size("tp")
    ny = n_tp // CORES
    far = nz // 2
    win = WINDOW
    units = 2 * far + 1
    tab = 8 * (far - win + 2)

    bf16, f32 = jnp.bfloat16, jnp.float32
    dma = pltpu.SemaphoreType.DMA
    hbm = pl.BlockSpec(memory_space=pltpu.HBM)
    smem = pl.BlockSpec(memory_space=pltpu.SMEM)
    mask = event_mask.reshape(-1, 1, EVENTS)
    who = cand_user.reshape(-1, DH)
    out = pl.pallas_call(
        functools.partial(kernel, (nz, nx, ny)),
        out_shape=pltpu.VMEM((CHUNKS, rows, DH), bf16),
        in_specs=[smem] * 3 + [hbm] * 6,
        out_specs=pl.BlockSpec(memory_space=pltpu.VMEM),
        scratch_shapes=[
            pltpu.VMEM(who.shape, jnp.int32),
            pltpu.VMEM(mask.shape, jnp.int32),
            pltpu.VMEM(kv_cache.shape, bf16),
            pltpu.VMEM((units, nx, CAP, EVENTS, 2 * DH), bf16),
            pltpu.VMEM((units, nx, CAP, EVENTS, 2 * DH), bf16),
            pltpu.VMEM((n_tp, CHUNKS, rows, DH), bf16),
            pltpu.VMEM(w_in.shape, bf16),
            pltpu.VMEM(w_out.shape, bf16),
            pltpu.VMEM((n_tp, DH, DH), bf16),
            pltpu.VMEM((nz * nx * CAP, DH), f32),
            pltpu.VMEM((2 * win + 1, tab, DH), f32),
            pltpu.VMEM((2 * win + 1, tab, DH), f32),
            pltpu.VMEM((2 * win + 1, CHUNKS, DH, rows), bf16),
            pltpu.VMEM((CHUNKS, rows, DH), bf16),
            pltpu.VMEM((DH, rows), bf16),
            pltpu.VMEM((2, win, CHUNKS, DH, rows), bf16),
            pltpu.VMEM((2, win, CHUNKS, DH, rows), bf16),
            pltpu.VMEM((n_tp, CHUNKS, rows, DH), bf16),
            dma((14,)),
            dma((units, nx)),
            dma((units, nx)),
            dma((2 * win + 1,)),
            dma((2 * win + 1,)),
            dma((CHUNKS, 2 * ny - 1)),
            dma((CHUNKS, 2 * ny - 1)),
            dma((CHUNKS, 2 * ny - 1)),
            dma((CHUNKS, 2 * ny - 1)),
            dma((n_tp,)),
            dma((n_tp,)),
            dma((2, win + 1, CHUNKS)),
            dma((2, win + 1, CHUNKS)),
            dma((2, win, CHUNKS)),
            dma((2, win, CHUNKS)),
        ],
        compiler_params=pltpu.CompilerParams(
            collective_id=0, has_side_effects=True, vmem_limit_bytes=60 * 2**20
        ),
        name="score",
    )(
        send_slots.T,
        block_counts,
        user_blocks,
        who,
        mask,
        kv_cache,
        cand_feats.reshape(CHUNKS, rows, DH),
        w_in,
        w_out,
    )
    return out.reshape(n_rows, DH)


def solution(mesh):
    in_specs = (
        P("user", "tp"),
        P(None, "tp"),
        P("tp", None),
        P("user", None, "tp"),
        P("user", None),
        P("user"),
        P("user", None),
        P("user", None),
        P("user"),
    )
    return jax.shard_map(
        functools.partial(per_device, Z_SIZE),
        mesh=mesh,
        in_specs=in_specs,
        out_specs=P("user", "tp"),
        check_vma=False,
    )
```

```python
import functools

import jax
import jax.numpy as jnp
from jax import lax
from jax.experimental import pallas as pl
from jax.experimental.pallas import tpu as pltpu
from jax.sharding import PartitionSpec as P

DH = 128
EVENTS = 128
CAP = 2
CORES = 2
Z_SIZE = 8
CHUNKS = 4
WINDOW = 3
norm_eps = 1e-06
FAR = -float(2**30)
HALF_SCALE = 0.5 * DH**-0.5
MESH = pl.DeviceIdType.MESH


def silu(v):
    x = 0.5 * v
    return x + x * jnp.tanh(x)


def kernel(
    dims,
    slots_ref,
    counts_ref,
    blocks_ref,
    who_hbm,
    mask_hbm,
    kv_hbm,
    feats_hbm,
    w_in_hbm,
    w_out_hbm,
    out_ref,
    who_v,
    mask_v,
    kv_v,
    snd,
    kvr,
    feats,
    w_in_v,
    w_out_v,
    w_out_all,
    ext_v,
    info_out,
    info_all,
    qs,
    gates,
    onehot,
    parts,
    incoming,
    hid,
    loc_sem,
    x_ss,
    x_rs,
    info_ss,
    info_rs,
    f_ss,
    f_rs,
    h_ss,
    h_rs,
    w_ss,
    w_rs,
    q_ss,
    q_rs,
    p_ss,
    p_rs,
):
    nz, nx, ny = dims
    far = nz // 2
    win = WINDOW
    rows = feats.shape[2]
    n_tp = ny * CORES
    n_blk = nx * CAP
    users, most = blocks_ref.shape
    me_u = lax.axis_index("user")
    me_t = lax.axis_index("tp")
    z, x = me_u // nx, me_u % nx
    y, core = me_t // CORES, me_t % CORES

    z_to = {d: ((z + d + nz) % nz * nx + x, me_t) for d in range(-win, win + 1)}
    x_to = [(z * nx + (x + j) % nx, me_t) for j in range(nx)]
    zx_to = {
        (d, j): ((z + d + nz) % nz * nx + (x + j) % nx, me_t)
        for d in range(win - far, far - win + 1) if d for j in range(nx)
    }
    partner = y * CORES + 1 - core
    y_to = [(me_u, partner)] + [(me_u, (y + j) % ny * CORES + core) for j in range(1, ny)]
    y_own = [(y - j + ny) % ny * CORES + core for j in range(ny)]
    y_other = [(y - j + ny) % ny * CORES + 1 - core for j in range(ny)]
    entries = [(x - j + nx) % nx * CAP for j in range(nx)]

    def at_z(d):
        return z_to[d]

    def at_x(j):
        return x_to[j]

    def at_t(t):
        return (me_u, t)

    def rc(src, dst, ss, rs, dev):
        return pltpu.make_async_remote_copy(
            src_ref=src, dst_ref=dst, send_sem=ss, recv_sem=rs,
            device_id=dev, device_id_type=MESH,
        )

    barrier = pltpu.get_barrier_semaphore()
    peers = [at_t((me_t + j) % n_tp) for j in range(1, n_tp)]
    peers += [at_x(j) for j in range(1, nx)]
    peers += [at_z(d * w) for d in range(1, win + 1) for w in (1, -1)]
    peers += [
        ((z + d * w + nz) % nz * nx + (x + j) % nx, me_t)
        for d in range(1, far - win + 1) for w in (1, -1) for j in range(1, nx)
    ]
    for dev in peers:
        pl.semaphore_signal(barrier, inc=1, device_id=dev, device_id_type=MESH)

    f_load = pltpu.make_async_copy(feats_hbm, feats.at[me_t], loc_sem.at[0])
    kv_step = kv_v.shape[0] // 8
    kv_loads = [
        pltpu.make_async_copy(kv_hbm.at[pl.ds(i * kv_step, kv_step)], kv_v.at[pl.ds(i * kv_step, kv_step)], loc_sem.at[6 + i])
        for i in range(8)
    ]
    wi_load = pltpu.make_async_copy(w_in_hbm, w_in_v, loc_sem.at[2])
    wo_load = pltpu.make_async_copy(w_out_hbm, w_out_v, loc_sem.at[3])
    mask_load = pltpu.make_async_copy(mask_hbm, mask_v, loc_sem.at[4])
    who_load = pltpu.make_async_copy(who_hbm, who_v, loc_sem.at[5])
    for load in [f_load, mask_load, *kv_loads, who_load, wi_load, wo_load]:
        load.start()

    onehot[...] = jnp.zeros_like(onehot)
    shape = (nz * n_blk, DH)
    slot_id = lax.broadcasted_iota(jnp.int32, shape, 0)
    lane = lax.broadcasted_iota(jnp.int32, shape, 1)
    ext = jnp.where(lane < users, FAR, 0.0)
    for u in range(users):
        hit = jnp.zeros(shape, jnp.bool_)
        for j in range(most):
            held = jnp.where(j < counts_ref[u], blocks_ref[u, j], -1)
            hit = jnp.logical_or(hit, slot_id == held)
        ext = jnp.where(jnp.logical_and(hit, lane == u), 0.0, ext)
    ext_v[...] = ext
    who_load.wait()
    who = who_v[...].astype(jnp.float32)

    def tables(ref, i, way, d):
        ref[i, 0 : who.shape[0]] = who
        for g in range(far - win + 1 if d == win else 1):
            holder = (z + (d + g) * (1 - 2 * way) + nz) % nz
            ref[i, 8 + 8 * g : 8 + 8 * g + n_blk] = ext_v[pl.ds(pl.multiple_of(holder * n_blk, n_blk), n_blk)]

    tables(info_all, 0, 0, 0)
    for way in range(2):
        for d in range(1, win + 1):
            tables(info_out, way * win + d, way, d)
    pl.semaphore_wait(barrier, len(peers))

    sends = []

    def go(copy):
        copy.start()
        sends.append(copy)

    def y_sends(buf, c, ss, rs, src=None):
        own = buf.at[me_t, c]
        src = own if src is None else src
        devs = y_to
        return [rc(src, own, ss.at[c, j], rs.at[c, j], devs[j]) for j in (2, 1, 3, 0)]

    def y_passed(buf, c, ss, rs, j, srcs):
        got = buf.at[srcs[j], c]
        k = ny - 1 + j if j else 0
        return rc(got, got, ss.at[c, k], rs.at[c, k], at_t(partner))

    def y_forward(buf, c, ss, rs):
        for j in range(1, ny):
            got = buf.at[y_own[j], c]
            rc(got, got, ss.at[c, j], rs.at[c, j], at_t(partner)).wait_recv()
            y_passed(buf, c, ss, rs, j, y_own).start()

    def y_wait(buf, c, ss, rs):
        for j in range(ny):
            y_passed(buf, c, ss, rs, j, y_other).wait_recv()

    def y_drain(buf, c, ss, rs):
        for copy in y_sends(buf, c, ss, rs):
            copy.wait_send()
        for j in range(1, ny):
            y_passed(buf, c, ss, rs, j, y_own).wait_send()

    for c in range(CHUNKS):
        for copy in y_sends(feats, c, f_ss, f_rs, feats_hbm.at[c]):
            copy.start()
    f_load.wait()

    def info_copy(i, dev):
        return rc(info_out.at[i], info_all.at[i], info_ss.at[i], info_rs.at[i], dev)

    for way in range(2):
        for d in range(1, win + 1):
            go(info_copy(way * win + d, at_z(d * (1 - 2 * way))))

    def unit(way, d):
        return jnp.maximum(2 * d - 1 + way, 0) if not isinstance(d, int) else (2 * d - 1 + way if d else 0)

    def x_copy(u, j):
        return rc(snd.at[u, j], kvr.at[u, j], x_ss.at[u, j], x_rs.at[u, j], at_x(j))

    def hop_copy(way, d, j):
        u = unit(way, d)
        dev = zx_to[(win - d) * (1 - 2 * way), j]
        if d < far:
            return rc(snd.at[u, j], kvr.at[u, j], x_ss.at[u, j], x_rs.at[u, j], dev)
        return rc(
            snd.at[2 * far - 1, j, way], kvr.at[u, j, way], x_ss.at[u, j], x_rs.at[u, j], dev
        )

    def prepare(n):
        way, d = (n + 1) % 2, far - (n + 1) // 2
        if isinstance(n, int) and d == far:
            way = 0
        u = unit(way, d)
        ranker = (z - d * (1 - 2 * way) + nz) % nz * nx

        def one(i, carry):
            j, c = i // CAP, i % CAP
            slot = slots_ref[c, ranker + (x + j) % nx]
            block = kv_v[slot]
            live = mask_v[slot].astype(jnp.float32).astype(jnp.bfloat16)
            snd[u, j, c, :, 0:DH] = block[:, 0:DH]
            snd[u, j, c, :, DH:] = block[:, DH:].T * live
            return carry

        lax.fori_loop(0, n_blk, one, 0, unroll=8)
        if isinstance(n, int) and d > win:
            for j in range(nx):
                for w in range(2) if d == far else (way,):
                    hop_copy(w, d, j).start()
        else:
            for j in range(1, nx):
                x_copy(u, j).start()

    def q_copy(way, d, c):
        before = 0 if d == 1 else way * win + d - 1
        return rc(
            qs.at[before, c], qs.at[way * win + d, c],
            q_ss.at[way, d, c], q_rs.at[way, d, c], z_to[1 - 2 * way if isinstance(way, int) else 1],
        )

    def inward(way):
        if isinstance(way, int):
            return z_to[2 * way - 1]
        return (jnp.where(way == 0, z_to[-1][0], z_to[1][0]), me_t)

    def p_copy(way, d, c):
        return rc(
            parts.at[way, d - 1, c], incoming.at[way, d - 1, c],
            p_ss.at[way, d - 1, c], p_rs.at[way, d - 1, c], inward(way),
        )

    def project(c):
        block = jnp.concatenate([feats[t, c] for t in range(n_tp)], axis=1)
        act = silu(jnp.dot(block, w_in_v[...], preferred_element_type=jnp.float32))
        qs[0, c] = act[:, 0:DH].T.astype(jnp.bfloat16)
        gates[c] = act[:, DH:].astype(jnp.bfloat16)

    def attend(i, c, blocks):
        user = lax.broadcasted_iota(jnp.int32, (16, DH), 0).astype(jnp.float32)
        per = rows // DH
        for r in range(per):
            row = info_all[i, pl.ds(c * per + r, 1), :]
            onehot[0:16, r * DH : (r + 1) * DH] = jnp.where(row == user, 1.0, 0.0).astype(jnp.bfloat16)
        keys, values = [], []
        for block, b in blocks:
            row = info_all[i, pl.ds(8 + b, 1), :].astype(jnp.bfloat16)
            keys.append(jnp.concatenate([block[:, 0:DH], jnp.broadcast_to(row, (EVENTS, DH))], axis=1))
            values.append(block[:, DH:])
        rhs = jnp.concatenate([qs[i, c], onehot[...]], axis=0)
        v = HALF_SCALE * jnp.dot(
            jnp.concatenate(keys, axis=0), rhs, preferred_element_type=jnp.float32
        )
        w = (v + v * jnp.tanh(v)).astype(jnp.bfloat16)
        return jnp.dot(jnp.concatenate(values, axis=1), w, preferred_element_type=jnp.float32)

    def entry(j, s):
        return entries[j] + s

    def near_blocks(u):
        return [
            (snd[u, 0, s] if j == 0 else kvr[u, j, s], entry(j, s)) for j in range(nx) for s in range(CAP)
        ]

    def edge_blocks(way):
        blocks = near_blocks(unit(way, win))
        for d in range(win + 1, far + 1):
            u = 2 * d - 1 + way
            for j in range(nx):
                if d < far:
                    blocks += [(kvr[u, j, s], 8 * (d - win) + entry(j, s)) for s in range(CAP)]
                else:
                    blocks += [(kvr[u, j, way], 8 * (d - win) + entry(j, way))]
        return blocks

    def in_range(c):
        return jnp.logical_and(c >= 0, c < CHUNKS)

    def tick(t, carry):
        @pl.when(t < CHUNKS)
        def _():
            y_wait(feats, t, f_ss, f_rs)
            project(t)
            for way in range(2):
                q_copy(way, 1, t).start()

        @pl.when(t + 1 < CHUNKS)
        def _():
            y_forward(feats, t + 1, f_ss, f_rs)

        for d in range(win - 1, 0, -1):
            c = t - d

            @pl.when(in_range(c))
            def _():
                for way in range(2):
                    q_copy(way, d, c).wait_recv()
                    q_copy(way, d + 1, c).start()

        c = t - win

        @pl.when(in_range(c))
        def _():
            def edge(way, carry):
                i = way * win + win

                @pl.when(c == 0)
                def _():
                    for j in range(1, nx):
                        x_copy(unit(way, win), j).wait_recv()
                    for d in range(win + 1, far + 1):
                        for j in range(nx):
                            got = kvr.at[2 * d - 1 + way, j]
                            if d == far:
                                got = got.at[way]
                            sems = x_ss.at[2 * d - 1 + way, j], x_rs.at[2 * d - 1 + way, j]
                            rc(got, got, *sems, at_x(1)).wait_recv()
                    info_copy(i, at_z(1)).wait_recv()

                q_copy(way, win, c).wait_recv()
                parts[way, win - 1, c] = attend(i, c, edge_blocks(way)).astype(jnp.bfloat16)
                p_copy(way, win, c).start()
                return carry

            lax.fori_loop(0, 2, edge, 0)

        return carry

    def inner(m, carry):
        d, c, way = win - 1 - m // (2 * CHUNKS), (m >> 1) & (CHUNKS - 1), m & 1
        u, i = 2 * d - 1 + way, way * win + d

        @pl.when(c == 0)
        def _():
            for j in range(1, nx):
                x_copy(u, j).wait_recv()
            info_copy(i, at_z(1)).wait_recv()

        total = attend(i, c, near_blocks(u))
        p_copy(way, d + 1, c).wait_recv()
        got = incoming[way, d, c].astype(jnp.float32)
        parts[way, d - 1, c] = (total + got).astype(jnp.bfloat16)
        p_copy(way, d, c).start()
        return carry

    def finish(c, carry):
        total = attend(0, c, near_blocks(0))
        for way in range(2):
            p_copy(way, 1, c).wait_recv()
            total = total + incoming[way, 0, c].astype(jnp.float32)
        inv = lax.rsqrt(jnp.mean(total * total, axis=0, keepdims=True) + norm_eps)
        normed = (total * inv).T * gates[c].astype(jnp.float32)
        hid[me_t, c] = normed.astype(jnp.bfloat16)
        for copy in y_sends(hid, c, h_ss, h_rs):
            copy.start()
        return carry

    def output(t, carry):
        @pl.when(t < CHUNKS)
        def _():
            y_forward(hid, t, h_ss, h_rs)
            for copy in y_sends(hid, t, h_ss, h_rs):
                copy.wait_send()
            for way in range(2):
                for d in range(1, win + 1):
                    p_copy(way, d, t).wait_send()

        @pl.when(t > 0)
        def _():
            c = t - 1
            y_wait(hid, c, h_ss, h_rs)
            block = jnp.concatenate([hid[s, c] for s in range(n_tp)], axis=1)
            w_all = jnp.concatenate([w_out_all[s] for s in range(n_tp)], axis=0)
            mixed = jnp.dot(block, w_all, preferred_element_type=jnp.float32)
            out_ref[c] = (feats[me_t, c].astype(jnp.float32) + mixed).astype(jnp.bfloat16)
            for j in range(1, ny):
                y_passed(hid, c, h_ss, h_rs, j, y_own).wait_send()

        return carry

    mask_load.wait()
    for load in kv_loads:
        load.wait()
    prepare(0)
    prepare(1)
    prepare(2)
    lax.fori_loop(3, 8, lambda n, carry: (prepare(n), carry)[1], 0)
    y_forward(feats, 0, f_ss, f_rs)
    wi_load.wait()
    wo_load.wait()
    w_out_all[me_t] = w_out_v[:, pl.ds(pl.multiple_of(me_t * DH, DH), DH)]
    for j in range(1, n_tp):
        s = (me_t + j) % n_tp
        cols = pl.ds(pl.multiple_of(s * DH, DH), DH)
        go(rc(w_out_v.at[:, cols], w_out_all.at[me_t], w_ss.at[j], w_rs.at[j], at_t(s)))
    lax.fori_loop(0, CHUNKS + win, tick, 0)
    lax.fori_loop(0, 2 * CHUNKS * (win - 1), inner, 0)
    for copy in sends:
        copy.wait_send()

    def drain_early(c, carry):
        y_drain(feats, c, f_ss, f_rs)
        for way in range(2):
            for d in range(1, win + 1):
                q_copy(way, d, c).wait_send()
        return carry

    lax.fori_loop(0, CHUNKS, drain_early, 0)
    for way in range(2):
        for d in range(win + 1, far + 1):
            for j in range(nx):
                hop_copy(way, d, j).wait_send()

    def drain_x(u, carry):
        for j in range(1, nx):
            x_copy(u, j).wait_send()
        return carry

    lax.fori_loop(1, 2 * win + 1, drain_x, 0)
    for j in range(1, n_tp):
        s = (me_t - j + n_tp) % n_tp
        rc(w_out_all.at[s], w_out_all.at[s], w_ss.at[j], w_rs.at[j], at_t(s)).wait_recv()
    for j in range(1, nx):
        x_copy(0, j).wait_recv()
    lax.fori_loop(0, CHUNKS, finish, 0)
    for j in range(1, nx):
        x_copy(0, j).wait_send()
    lax.fori_loop(0, CHUNKS + 1, output, 0)


def per_device(
    nz, cand_feats, w_in, w_out, kv_cache, event_mask, block_counts, user_blocks, send_slots, cand_user
):
    n_rows = cand_feats.shape[0]
    rows = n_rows // CHUNKS
    nx = lax.axis_size("user") // nz
    n_tp = lax.axis_size("tp")
    ny = n_tp // CORES
    far = nz // 2
    win = WINDOW
    units = 2 * far + 1
    tab = 8 * (far - win + 2)

    bf16, f32 = jnp.bfloat16, jnp.float32
    dma = pltpu.SemaphoreType.DMA
    hbm = pl.BlockSpec(memory_space=pltpu.HBM)
    smem = pl.BlockSpec(memory_space=pltpu.SMEM)
    mask = event_mask.reshape(-1, 1, EVENTS)
    who = cand_user.reshape(-1, DH)
    out = pl.pallas_call(
        functools.partial(kernel, (nz, nx, ny)),
        out_shape=pltpu.VMEM((CHUNKS, rows, DH), bf16),
        in_specs=[smem] * 3 + [hbm] * 6,
        out_specs=pl.BlockSpec(memory_space=pltpu.VMEM),
        scratch_shapes=[
            pltpu.VMEM(who.shape, jnp.int32),
            pltpu.VMEM(mask.shape, jnp.int32),
            pltpu.VMEM(kv_cache.shape, bf16),
            pltpu.VMEM((units, nx, CAP, EVENTS, 2 * DH), bf16),
            pltpu.VMEM((units, nx, CAP, EVENTS, 2 * DH), bf16),
            pltpu.VMEM((n_tp, CHUNKS, rows, DH), bf16),
            pltpu.VMEM(w_in.shape, bf16),
            pltpu.VMEM(w_out.shape, bf16),
            pltpu.VMEM((n_tp, DH, DH), bf16),
            pltpu.VMEM((nz * nx * CAP, DH), f32),
            pltpu.VMEM((2 * win + 1, tab, DH), f32),
            pltpu.VMEM((2 * win + 1, tab, DH), f32),
            pltpu.VMEM((2 * win + 1, CHUNKS, DH, rows), bf16),
            pltpu.VMEM((CHUNKS, rows, DH), bf16),
            pltpu.VMEM((DH, rows), bf16),
            pltpu.VMEM((2, win, CHUNKS, DH, rows), bf16),
            pltpu.VMEM((2, win, CHUNKS, DH, rows), bf16),
            pltpu.VMEM((n_tp, CHUNKS, rows, DH), bf16),
            dma((14,)),
            dma((units, nx)),
            dma((units, nx)),
            dma((2 * win + 1,)),
            dma((2 * win + 1,)),
            dma((CHUNKS, 2 * ny - 1)),
            dma((CHUNKS, 2 * ny - 1)),
            dma((CHUNKS, 2 * ny - 1)),
            dma((CHUNKS, 2 * ny - 1)),
            dma((n_tp,)),
            dma((n_tp,)),
            dma((2, win + 1, CHUNKS)),
            dma((2, win + 1, CHUNKS)),
            dma((2, win, CHUNKS)),
            dma((2, win, CHUNKS)),
        ],
        compiler_params=pltpu.CompilerParams(
            collective_id=0, has_side_effects=True, vmem_limit_bytes=60 * 2**20
        ),
        name="score",
    )(
        send_slots.T,
        block_counts,
        user_blocks,
        who,
        mask,
        kv_cache,
        cand_feats.reshape(CHUNKS, rows, DH),
        w_in,
        w_out,
    )
    return out.reshape(n_rows, DH)


def solution(mesh):
    in_specs = (
        P("user", "tp"),
        P(None, "tp"),
        P("tp", None),
        P("user", None, "tp"),
        P("user", None),
        P("user"),
        P("user", None),
        P("user", None),
        P("user"),
    )
    return jax.shard_map(
        functools.partial(per_device, Z_SIZE),
        mesh=mesh,
        in_specs=in_specs,
        out_specs=P("user", "tp"),
        check_vma=False,
    )
```
